32 devices in a mesh: ctx: 16 (over z, x, core), tp: 2 (over y).
Axes of the slice: x: 2, y: 2, z: 4, core: 2. Of those that a mesh axis runs over, the one named last changes fastest.
Arguments:
- inputs: bfloat16 [3, 2048, 4096], P(None, 'ctx', 'tp'), may hold values from -6 to 6
- short_weight: float32 [3, 3, 4096], P(None, None, 'tp'), may hold values from -3 to 3
- taps: float32 [2048, 4096], P('ctx', 'tp'), may hold values from -6 to 6
- w_out: bfloat16 [4096, 4096], P('tp'), may hold values from -0.09375 to 0.09375
- grad_out: bfloat16 [2048, 4096], P('ctx', 'tp'), may hold values from -6 to 6
Outputs:
- inputs_grad: bfloat16 [3, 2048, 4096], P(None, 'ctx', 'tp')
- taps_grad: float32 [2048, 4096], P('ctx', 'tp')
- short_grad: float32 [3, 3, 4096], P(None, None, 'tp')
The draws below stay inside these ranges and needn't reach their ends.
All inputs are finite; a program needn't handle non-finite values.
Results may differ from the reference program's by a relative error of at most 0.0015.
Values may be sent and summed in bfloat16 or wider, within the bound.
A program may use at most 192 MiB of HBM per device.

```python
import math
import jax
import jax.numpy as jnp
from jax import lax

D = 4096
SHORT = 3
SEQ = 2048


def levels(own_key, shape, pieces, low, largest):
    level, own = 1.0, jax.random.fold_in(own_key, 6)
    for position, blocks in pieces:
        draws = jnp.exp(jax.random.uniform(jax.random.fold_in(own, position), (blocks,), jnp.float32, low / len(pieces), largest / len(pieces)))
        level = level * jnp.repeat(draws, shape[position] // blocks).reshape([-1 if axis == position else 1 for axis in range(len(shape))])
    return level


def gaussian(rng, shape, scale, bound, shards=(), kind=jnp.bfloat16):
    loudness = levels(rng, shape, shards, -0.22, 0.18) if shards else 1.0
    drawn = jax.random.normal(rng, shape, jnp.float32) * scale * loudness
    return jnp.minimum(jnp.maximum(drawn, -bound), bound).astype(kind)


def setup_inputs(seed: int = 0) -> dict:
    splits = jax.random.split(jax.random.key(seed), 6)
    inputs = gaussian(splits[0], (3, SEQ, D), 1.0, 6.0, ((1, 16), (2, 2)))
    short_weight = gaussian(splits[1], (3, SHORT, D), 0.6, 3.0, ((2, 2),), jnp.float32)
    taps = gaussian(splits[2], (SEQ, D), 1.0, 6.0, ((0, 16), (1, 2)), jnp.float32)
    w_out = gaussian(splits[3], (D, D), D ** -0.5, 0.09375, ((0, 2),))
    grad_out = gaussian(splits[4], (SEQ, D), 1.0, 6.0, ((0, 16), (1, 2)))
    return dict(inputs=inputs, short_weight=short_weight, taps=taps, w_out=w_out, grad_out=grad_out)


def causal_mix(streams, weight):
    length = streams.shape[1]
    span = weight.shape[1]
    padded = jnp.concatenate([jnp.zeros_like(streams[:, :span - 1]), streams], axis=1)
    total = jnp.zeros_like(streams)
    for j in range(span):
        total = total + weight[:, j][:, None, :] * padded[:, span - 1 - j:span - 1 - j + length]
    return (total, padded)

def spectral_block(block):
    length = block.shape[1]
    spec = jnp.fft.rfft(block, n=2 * length, axis=1)
    filt, prod, grad = (spec[0], spec[1], spec[2])
    joined = jnp.stack([filt * prod, jnp.conj(filt) * grad, jnp.conj(prod) * grad])
    return jnp.fft.irfft(joined, n=2 * length, axis=1)[:, :length]

def reference(inputs, short_weight, taps, w_out, grad_out):
    scale = 1.0 / math.sqrt(SEQ)
    streams = inputs.astype(jnp.float32)
    mixed, padded = causal_mix(streams, short_weight)
    query, key_s, value = (mixed[0], mixed[1], mixed[2])
    product = key_s * value
    filt = taps * scale
    gated_grad = jnp.dot(grad_out, w_out.T, preferred_element_type=jnp.float32)
    dy = gated_grad * query
    width = min(256, D)
    stacked = jnp.stack([filt, product, dy]).reshape(3, SEQ, D // width, width).transpose(2, 0, 1, 3)
    result = lax.map(spectral_block, stacked)
    result = result.transpose(1, 2, 0, 3).reshape(3, SEQ, D)
    conv_out, dz, raw = (result[0], result[1], result[2])
    dmixed = jnp.stack([gated_grad * conv_out, dz * value, dz * key_s])
    span = SHORT
    dpad = jnp.concatenate([dmixed, jnp.zeros_like(dmixed[:, :span - 1])], axis=1)
    inputs_grad = jnp.zeros_like(dmixed)
    sums = []
    for j in range(span):
        inputs_grad = inputs_grad + short_weight[:, j][:, None, :] * dpad[:, j:j + SEQ]
        sums.append(lax.optimization_barrier(jnp.sum(dmixed * padded[:, span - 1 - j:span - 1 - j + SEQ], axis=1)))
    short_grad = jnp.stack(sums, axis=1) * scale
    return (inputs_grad.astype(jnp.bfloat16), raw * scale, short_grad)
```

```python
import functools
import math

import jax
import jax.numpy as jnp
import numpy as np
from jax import lax
from jax.experimental import pallas as pl
from jax.experimental.pallas import tpu as pltpu
from jax.sharding import PartitionSpec as P

HIGH = lax.Precision.HIGHEST
MESH = pl.DeviceIdType.MESH
FINE = 256
TOP = 248.0 * 128.0 - 1.0


def shifted(x, axis, by):
    peers = lax.axis_size(axis)
    pairs = [(i, i + by) for i in range(peers) if 0 <= i + by < peers]
    return lax.ppermute(x, axis, pairs)


def phase(left_idx, right_idx, period):
    turns = left_idx[:, None] * right_idx[None, :] % period
    angle = turns.astype(jnp.float32) * (2.0 * math.pi / period)
    return (jnp.cos(angle), jnp.sin(angle))


def section_one(blocks, n2_start, period):
    count = blocks.shape[1]
    width = blocks.shape[2]
    cos_a, sin_a = phase(
        jnp.arange(2 * count, dtype=jnp.int32), jnp.arange(count, dtype=jnp.int32), 2 * count
    )
    real_part = jnp.einsum("kn,bnmc->bkmc", cos_a, blocks, precision=HIGH)
    imag_part = -jnp.einsum("kn,bnmc->bkmc", sin_a, blocks, precision=HIGH)
    cos_b, sin_b = phase(
        jnp.arange(2 * count, dtype=jnp.int32),
        n2_start + jnp.arange(width, dtype=jnp.int32),
        period,
    )
    tw_re = cos_b[None, :, :, None]
    tw_im = -sin_b[None, :, :, None]
    return jnp.stack([real_part * tw_re - imag_part * tw_im, real_part * tw_im + imag_part * tw_re])


def section_two(parts):
    length = parts.shape[3]
    cos_a, sin_a = phase(
        jnp.arange(length, dtype=jnp.int32), jnp.arange(length, dtype=jnp.int32), length
    )
    real_in, imag_in = (parts[0], parts[1])
    cc_re = jnp.einsum("qn,bknc->bkqc", cos_a, real_in, precision=HIGH)
    cc_im = jnp.einsum("qn,bknc->bkqc", cos_a, imag_in, precision=HIGH)
    ss_re = jnp.einsum("qn,bknc->bkqc", sin_a, real_in, precision=HIGH)
    ss_im = jnp.einsum("qn,bknc->bkqc", sin_a, imag_in, precision=HIGH)
    return jnp.stack([cc_re + ss_im, cc_im - ss_re])


def inverse_two(spec, k1_start, period):
    classes = spec.shape[2]
    length = spec.shape[3]
    cos_a, sin_a = phase(
        jnp.arange(length, dtype=jnp.int32), jnp.arange(length, dtype=jnp.int32), length
    )
    real_in, imag_in = (spec[0], spec[1])
    cc_re = jnp.einsum("nq,bkqc->bknc", cos_a, real_in, precision=HIGH)
    cc_im = jnp.einsum("nq,bkqc->bknc", cos_a, imag_in, precision=HIGH)
    ss_re = jnp.einsum("nq,bkqc->bknc", sin_a, real_in, precision=HIGH)
    ss_im = jnp.einsum("nq,bkqc->bknc", sin_a, imag_in, precision=HIGH)
    back_re = cc_re - ss_im
    back_im = cc_im + ss_re
    cos_b, sin_b = phase(
        k1_start + jnp.arange(classes, dtype=jnp.int32), jnp.arange(length, dtype=jnp.int32), period
    )
    tw_re = cos_b[None, :, :, None]
    tw_im = sin_b[None, :, :, None]
    return jnp.stack([back_re * tw_re - back_im * tw_im, back_re * tw_im + back_im * tw_re])


def inverse_one(spec, period):
    classes = spec.shape[2]
    count = classes // 2
    cos_a, sin_a = phase(
        jnp.arange(count, dtype=jnp.int32), jnp.arange(classes, dtype=jnp.int32), classes
    )
    real_out = jnp.einsum("nk,bkmc->bnmc", cos_a, spec[0], precision=HIGH)
    real_out = real_out - jnp.einsum("nk,bkmc->bnmc", sin_a, spec[1], precision=HIGH)
    return real_out / period


def products(spec):
    filt_re, filt_im = (spec[0, 0], spec[1, 0])
    prod_re, prod_im = (spec[0, 1], spec[1, 1])
    grad_re, grad_im = (spec[0, 2], spec[1, 2])
    out_re = jnp.stack(
        [
            filt_re * prod_re - filt_im * prod_im,
            filt_re * grad_re + filt_im * grad_im,
            prod_re * grad_re + prod_im * grad_im,
        ]
    )
    out_im = jnp.stack(
        [
            filt_re * prod_im + filt_im * prod_re,
            filt_re * grad_im - filt_im * grad_re,
            prod_re * grad_im - prod_im * grad_re,
        ]
    )
    return jnp.stack([out_re, out_im])


def shards(inputs, short_weight, taps, w_out, grad_out):
    rows = inputs.shape[1]
    span = short_weight.shape[1]
    count = lax.axis_size("ctx")
    where = lax.axis_index("ctx")
    period = 2 * count * rows
    scale = 1.0 / math.sqrt(count * rows)
    prior = shifted(inputs[:, rows - (span - 1) :, :], "ctx", 1)
    extended = jnp.concatenate([prior, inputs], axis=1).astype(jnp.float32)
    mixed = jnp.zeros((3, rows, inputs.shape[2]), jnp.float32)
    for j in range(span):
        mixed = (
            mixed + short_weight[:, j][:, None, :] * extended[:, span - 1 - j : span - 1 - j + rows]
        )
    query, key_s, value = (mixed[0], mixed[1], mixed[2])
    product = key_s * value
    filt = taps * scale
    columns = w_out
    gated_grad = lax.dot_general(
        lax.all_gather(grad_out, "tp", axis=1, tiled=True),
        columns,
        (((1,), (1,)), ((), ())),
        preferred_element_type=jnp.float32,
    )
    dy = gated_grad * query
    stacked = jnp.stack([filt, product, dy])
    width = rows // count
    blocks = stacked.reshape(3, count, width, stacked.shape[2])
    columns = section_one(
        lax.all_to_all(blocks, "ctx", split_axis=1, concat_axis=1, tiled=True),
        n2_start=where * width,
        period=period,
    )
    spec = section_two(lax.all_to_all(columns, "ctx", split_axis=2, concat_axis=3, tiled=True))
    back = inverse_two(products(spec), where * spec.shape[2], period)
    parted = inverse_one(
        lax.all_to_all(back, "ctx", split_axis=3, concat_axis=2, tiled=True), period=period
    )
    result = lax.all_to_all(parted, "ctx", split_axis=1, concat_axis=1, tiled=True).reshape(
        3, rows, stacked.shape[2]
    )
    conv_out, dz, raw = (result[0], result[1], result[2])
    dmixed = jnp.stack([gated_grad * conv_out, dz * value, dz * key_s])
    following = shifted(dmixed[:, : span - 1, :].astype(jnp.bfloat16), "ctx", -1).astype(
        jnp.float32
    )
    dext = jnp.concatenate([dmixed, following], axis=1)
    inputs_grad = jnp.zeros_like(dmixed)
    sums = []
    for j in range(span):
        inputs_grad = inputs_grad + short_weight[:, j][:, None, :] * dext[:, j : j + rows]
        sums.append(jnp.sum(dmixed * extended[:, span - 1 - j : span - 1 - j + rows], axis=1))
    short_grad = lax.psum(jnp.stack(sums, axis=1), "ctx") * scale
    return (inputs_grad.astype(jnp.bfloat16), raw * scale, short_grad)


def log2(x):
    return jnp.log(x) * (1.0 / math.log(2.0))


def encode(x):
    peak = jnp.maximum(jnp.max(jnp.abs(x), axis=0, keepdims=True), 1e-30)
    power = jnp.ceil(log2(peak))
    level = jnp.floor(jnp.abs(x) * (jnp.exp2(-power) * TOP) + 0.5)
    level = jnp.minimum(level, TOP)
    octave = jnp.floor(level * (1.0 / 128.0))
    size = jnp.exp2(octave - 123.0) * (1.0 + (level - octave * 128.0) * (1.0 / 128.0))
    return jnp.where(x < 0.0, -size, size).astype(jnp.bfloat16), power


def decode(words, power):
    words = words.astype(jnp.float32)
    size = jnp.abs(words)
    octave = jnp.floor(log2(size) + 0.0014)
    part = jnp.floor(size * jnp.exp2(-octave) * 128.0 + 0.5)
    level = octave * 128.0 + part + (123.0 * 128.0 - 128.0)
    return jnp.where(words < 0.0, -level, level) * (jnp.exp2(power.astype(jnp.float32)) / TOP)


def rows_of(powers):
    row = lax.broadcasted_iota(jnp.int32, (16, powers[0].shape[1]), 0)
    rows = jnp.where(row == 0, powers[0], jnp.where(row == 1, powers[1], powers[2]))
    return rows.astype(jnp.bfloat16)


def split(x):
    high = x.astype(jnp.bfloat16)
    return high, (x - high.astype(jnp.float32)).astype(jnp.bfloat16)


def product3(m_high, m_low, x):
    x_high, x_low = split(x)
    dot = lambda a, b: jnp.dot(a, b, preferred_element_type=jnp.float32)
    return dot(m_high, x_high) + (dot(m_low, x_high) + dot(m_high, x_low))


def times_root(z, k, count, sign):
    re, im = z
    k = k % count
    if 8 * k % count == 0:
        turn = 8 * k // count
        if turn % 2 == 0:
            for _ in range(turn // 2):
                re, im = (im, -re) if sign < 0 else (-im, re)
            return re, im
    c, s = math.cos(2 * math.pi * k / count), sign * math.sin(2 * math.pi * k / count)
    if 8 * k % count == 0:
        r = abs(c)
        if (c > 0) == (s > 0):
            out = (re - im) * r, (re + im) * r
        else:
            out = (re + im) * r, (im - re) * r
        return out if c > 0 else (-out[0], -out[1])
    return re * c - im * s, re * s + im * c


def small_dft(z, sign):
    count = len(z)
    if count == 1:
        return z
    even, odd = small_dft(z[0::2], sign), small_dft(z[1::2], sign)
    odd = [times_root(v, k, count, sign) for k, v in enumerate(odd)]
    return [(a[0] + b[0], a[1] + b[1]) for a, b in zip(even, odd)] + [
        (a[0] - b[0], a[1] - b[1]) for a, b in zip(even, odd)
    ]


def matrices(length):
    radix = length // FINE
    k = np.arange(FINE)[None, :, None] + 0.25
    n = radix * np.arange(FINE)[None, None, :] + np.arange(radix)[:, None, None]
    angle = -2.0 * np.pi * k * n / length
    forward = np.concatenate([np.cos(angle), np.sin(angle)], axis=1).astype(np.float32)

    def halves(m):
        high = m.astype(jnp.bfloat16)
        return np.stack([high, (m - high.astype(np.float32)).astype(jnp.bfloat16)])

    return halves(forward), halves(np.ascontiguousarray(forward.transpose(0, 2, 1)))


def transform_products(xs, ys, f_ref, ft_ref, factor):
    length, lanes = xs.shape[1], xs.shape[2]
    radix = length // FINE
    for n2 in range(radix):
        x = jnp.concatenate([xs[a, pl.ds(n2, FINE, stride=radix), :] for a in range(3)], axis=1)
        ys[n2] = product3(f_ref[0, n2], f_ref[1, n2], x)

    def spectra(t, _):
        row = pl.multiple_of(t * 8, 8)
        specs = []
        for a in range(3):
            cols = pl.ds(a * lanes, lanes)
            z = [
                (ys[n2, pl.ds(row, 8), cols], ys[n2, pl.ds(FINE + row, 8), cols])
                for n2 in range(radix)
            ]
            specs.append(small_dft(z, -1))
        filt, prod, grad = specs
        joined = [[], [], []]
        for (fr, fi), (pr, pi), (gr, gi) in zip(filt, prod, grad):
            joined[0].append((fr * pr - fi * pi, fr * pi + fi * pr))
            joined[1].append((fr * gr + fi * gi, fr * gi - fi * gr))
            joined[2].append((pr * gr + pi * gi, pr * gi - pi * gr))
        for a in range(3):
            cols = pl.ds(a * lanes, lanes)
            for n2, (re, im) in enumerate(small_dft(joined[a], 1)):
                ys[n2, pl.ds(row, 8), cols] = re * factor
                ys[n2, pl.ds(FINE + row, 8), cols] = im * factor
        return 0

    lax.fori_loop(0, FINE // 8, spectra, 0)
    for n2 in range(radix):
        x = product3(ft_ref[0, n2], ft_ref[1, n2], ys[n2])
        for a in range(3):
            xs[a, pl.ds(n2, FINE, stride=radix), :] = x[:, a * lanes : (a + 1) * lanes]


def greet(count):
    me = lax.axis_index("ctx")
    barrier = pltpu.get_barrier_semaphore()
    for s in range(1, count):
        pl.semaphore_signal(
            barrier, inc=1, device_id={"ctx": lax.rem(me + s, count)}, device_id_type=MESH
        )
    pl.semaphore_wait(barrier, count - 1)
    return me


def remote(src, dst, send_sem, recv_sem, peer):
    return pltpu.make_async_remote_copy(
        src_ref=src,
        dst_ref=dst,
        send_sem=send_sem,
        recv_sem=recv_sem,
        device_id={"ctx": peer},
        device_id_type=MESH,
    )


def conv_kernel(
    count, factor, h_ref, z_ref, g_ref, f_hbm, ft_hbm, y_ref, dz_ref, raw_ref,
    there, arrived, back, returned, xs, ys, f_ref, ft_ref, local_sem, send_sem, recv_sem,
):
    rows, lanes = xs.shape[1] // count, xs.shape[2]
    me = greet(count)
    loads = [
        pltpu.make_async_copy(f_hbm, f_ref, local_sem.at[0]),
        pltpu.make_async_copy(ft_hbm, ft_ref, local_sem.at[1]),
    ]
    for load in loads:
        load.start()

    def columns(d):
        return pl.ds(pl.multiple_of(d * lanes, lanes), lanes)

    def fill(buf, d, parts):
        powers = []
        for a, x in enumerate(parts):
            words, power = encode(x)
            buf[d, pl.ds(a * rows, rows), :] = words
            powers.append(power)
        buf[d, pl.ds(3 * rows, 16), :] = rows_of(powers)

    def sending(src, dst, phase, s):
        peer = lax.rem(me + s, count)
        return remote(
            src.at[peer], dst.at[me], send_sem.at[phase, s], recv_sem.at[phase, s], peer
        )

    def landing(src, dst, phase, s):
        peer = lax.rem(me + count - s, count)
        return remote(
            src.at[peer], dst.at[peer], send_sem.at[phase, s], recv_sem.at[phase, s], peer
        )

    order = list(range(1, count)) + [0]
    for s in order:
        d = lax.rem(me + s, count)
        fill(there, d, [ref[:, columns(d)] for ref in (h_ref, z_ref, g_ref)])
        if s:
            sending(there, arrived, 0, s).start()

    for s in range(count):
        d = lax.rem(me + count - s, count)
        if s:
            landing(there, arrived, 0, s).wait_recv()
        block = there[d] if s == 0 else arrived[d]
        powers = block[3 * rows :].astype(jnp.float32)
        for a in range(3):
            xs[a, pl.ds(pl.multiple_of(d * rows, rows), rows), :] = decode(
                block[a * rows : (a + 1) * rows], powers[a : a + 1]
            )
    for load in loads:
        load.wait()
    transform_products(xs, ys, f_ref, ft_ref, factor)

    for s in order:
        d = lax.rem(me + s, count)
        at = pl.ds(pl.multiple_of(d * rows, rows), rows)
        fill(back, d, [xs[a, at, :] for a in range(3)])
        if s:
            sending(back, returned, 1, s).start()
    for s in range(count):
        d = lax.rem(me + count - s, count)
        if s:
            landing(back, returned, 1, s).wait_recv()
        block = back[d] if s == 0 else returned[d]
        powers = block[3 * rows :].astype(jnp.float32)
        for a, ref in enumerate((y_ref, dz_ref, raw_ref)):
            ref[:, columns(d)] = decode(block[a * rows : (a + 1) * rows], powers[a : a + 1])
    for s in range(1, count):
        sending(there, arrived, 0, s).wait_send()
        sending(back, returned, 1, s).wait_send()


def convolve(taps, product, dy, count, scale):
    rows, width = taps.shape
    lanes = width // count
    length = rows * count
    radix = length // FINE
    forward, backward = matrices(length)
    vmem, anywhere = pl.BlockSpec(memory_space=pltpu.VMEM), pl.BlockSpec(memory_space=pl.ANY)
    block = (count, 3 * rows + 16, lanes)
    return pl.pallas_call(
        functools.partial(conv_kernel, count, scale / length),
        out_shape=[jax.ShapeDtypeStruct((rows, width), jnp.float32)] * 3,
        in_specs=[vmem, vmem, vmem, anywhere, anywhere],
        out_specs=[vmem] * 3,
        scratch_shapes=[pltpu.VMEM(block, jnp.bfloat16)] * 4
        + [
            pltpu.VMEM((3, length, lanes), jnp.float32),
            pltpu.VMEM((radix, 2 * FINE, 3 * lanes), jnp.float32),
            pltpu.VMEM(forward.shape, jnp.bfloat16),
            pltpu.VMEM(backward.shape, jnp.bfloat16),
            pltpu.SemaphoreType.DMA((2,)),
            pltpu.SemaphoreType.DMA((2, count)),
            pltpu.SemaphoreType.DMA((2, count)),
        ],
        compiler_params=pltpu.CompilerParams(
            collective_id=0, has_side_effects=True, vmem_limit_bytes=56 * 2**20
        ),
        cost_estimate=pl.CostEstimate(
            flops=36 * length * FINE * 3 * lanes, bytes_accessed=24 * rows * width, transcendentals=0
        ),
        name="long_convolution",
    )(taps, product, dy, jnp.asarray(forward), jnp.asarray(backward))


def sum_kernel(count, part_ref, out_ref, arrived, total, send_sem, recv_sem):
    me = greet(count)

    def copy(phase, s, mine):
        peer = lax.rem(me + (s if mine else count - s), count)
        src = part_ref.at[peer] if phase == 0 else total
        dst = (arrived if phase == 0 else out_ref).at[me if mine else peer]
        return remote(src, dst, send_sem.at[phase, s], recv_sem.at[phase, s], peer)

    for s in range(1, count):
        copy(0, s, True).start()
    value = part_ref[me]
    for s in range(1, count):
        copy(0, s, False).wait_recv()
        value = value + arrived[lax.rem(me + count - s, count)]
    total[...] = value
    for s in range(1, count):
        copy(1, s, True).start()
    out_ref[me] = value
    for s in range(1, count):
        copy(1, s, False).wait_recv()
    for s in range(1, count):
        copy(0, s, True).wait_send()
        copy(1, s, True).wait_send()


def summed(part, count):
    lead, width = part.shape
    lanes = width // count
    padded = -(-lead // 8) * 8
    blocks = jnp.pad(part, ((0, padded - lead), (0, 0)))
    blocks = blocks.reshape(padded, count, lanes).transpose(1, 0, 2)
    vmem = pl.BlockSpec(memory_space=pltpu.VMEM)
    total = pl.pallas_call(
        functools.partial(sum_kernel, count),
        out_shape=jax.ShapeDtypeStruct(blocks.shape, jnp.float32),
        in_specs=[vmem],
        out_specs=vmem,
        scratch_shapes=[
            pltpu.VMEM(blocks.shape, jnp.float32),
            pltpu.VMEM(blocks.shape[1:], jnp.float32),
            pltpu.SemaphoreType.DMA((2, count)),
            pltpu.SemaphoreType.DMA((2, count)),
        ],
        compiler_params=pltpu.CompilerParams(collective_id=1, has_side_effects=True),
        name="tap_sums",
    )(blocks)
    return total.transpose(1, 0, 2).reshape(padded, width)[:lead]


def channel_shards(inputs, short_weight, taps, w_out, grad_out):
    rows, width = taps.shape
    span = short_weight.shape[1]
    count = lax.axis_size("ctx")
    scale = 1.0 / math.sqrt(count * rows)
    prior = shifted(inputs[:, rows - (span - 1) :, :], "ctx", 1)
    extended = jnp.concatenate([prior, inputs], axis=1).astype(jnp.float32)
    mixed = jnp.zeros((3, rows, width), jnp.float32)
    for j in range(span):
        mixed = (
            mixed + short_weight[:, j][:, None, :] * extended[:, span - 1 - j : span - 1 - j + rows]
        )
    query, key_s, value = (mixed[0], mixed[1], mixed[2])
    gated_grad = lax.dot_general(
        lax.all_gather(grad_out, "tp", axis=1, tiled=True),
        w_out,
        (((1,), (1,)), ((), ())),
        preferred_element_type=jnp.float32,
    )
    conv_out, dz, taps_grad = convolve(taps, key_s * value, gated_grad * query, count, scale)
    dmixed = jnp.stack([gated_grad * conv_out, dz * value, dz * key_s])
    following = shifted(dmixed[:, : span - 1, :].astype(jnp.bfloat16), "ctx", -1).astype(
        jnp.float32
    )
    dext = jnp.concatenate([dmixed, following], axis=1)
    inputs_grad = jnp.zeros_like(dmixed)
    sums = []
    for j in range(span):
        inputs_grad = inputs_grad + short_weight[:, j][:, None, :] * dext[:, j : j + rows]
        sums.append(jnp.sum(dmixed * extended[:, span - 1 - j : span - 1 - j + rows], axis=1))
    part = jnp.stack(sums, axis=1).reshape(3 * span, width) * scale
    short_grad = summed(part, count).reshape(3, span, width)
    return (inputs_grad.astype(jnp.bfloat16), taps_grad, short_grad)


def any_shards(inputs, short_weight, taps, w_out, grad_out):
    rows, width = taps.shape
    count = lax.axis_size("ctx")
    whole_tiles = rows % 16 == 0 and width % (128 * count) == 0 and rows * count == 8 * FINE
    plan = channel_shards if whole_tiles else shards
    return plan(inputs, short_weight, taps, w_out, grad_out)


def solution(mesh):
    return jax.shard_map(
        any_shards,
        mesh=mesh,
        in_specs=(
            P(None, "ctx", "tp"),
            P(None, None, "tp"),
            P("ctx", "tp"),
            P("tp", None),
            P("ctx", "tp"),
        ),
        out_specs=(P(None, "ctx", "tp"), P("ctx", "tp"), P(None, None, "tp")),
        check_vma=False,
    )
```

```python
import functools
import math

import jax
import jax.numpy as jnp
import numpy as np
from jax import lax
from jax.experimental import pallas as pl
from jax.experimental.pallas import tpu as pltpu
from jax.sharding import PartitionSpec as P

HIGH = lax.Precision.HIGHEST
MESH = pl.DeviceIdType.MESH
FINE = 256
TOP = 248.0 * 128.0 - 1.0


def shifted(x, axis, by):
    peers = lax.axis_size(axis)
    pairs = [(i, i + by) for i in range(peers) if 0 <= i + by < peers]
    return lax.ppermute(x, axis, pairs)


def phase(left_idx, right_idx, period):
    turns = left_idx[:, None] * right_idx[None, :] % period
    angle = turns.astype(jnp.float32) * (2.0 * math.pi / period)
    return (jnp.cos(angle), jnp.sin(angle))


def section_one(blocks, n2_start, period):
    count = blocks.shape[1]
    width = blocks.shape[2]
    cos_a, sin_a = phase(
        jnp.arange(2 * count, dtype=jnp.int32), jnp.arange(count, dtype=jnp.int32), 2 * count
    )
    real_part = jnp.einsum("kn,bnmc->bkmc", cos_a, blocks, precision=HIGH)
    imag_part = -jnp.einsum("kn,bnmc->bkmc", sin_a, blocks, precision=HIGH)
    cos_b, sin_b = phase(
        jnp.arange(2 * count, dtype=jnp.int32),
        n2_start + jnp.arange(width, dtype=jnp.int32),
        period,
    )
    tw_re = cos_b[None, :, :, None]
    tw_im = -sin_b[None, :, :, None]
    return jnp.stack([real_part * tw_re - imag_part * tw_im, real_part * tw_im + imag_part * tw_re])


def section_two(parts):
    length = parts.shape[3]
    cos_a, sin_a = phase(
        jnp.arange(length, dtype=jnp.int32), jnp.arange(length, dtype=jnp.int32), length
    )
    real_in, imag_in = (parts[0], parts[1])
    cc_re = jnp.einsum("qn,bknc->bkqc", cos_a, real_in, precision=HIGH)
    cc_im = jnp.einsum("qn,bknc->bkqc", cos_a, imag_in, precision=HIGH)
    ss_re = jnp.einsum("qn,bknc->bkqc", sin_a, real_in, precision=HIGH)
    ss_im = jnp.einsum("qn,bknc->bkqc", sin_a, imag_in, precision=HIGH)
    return jnp.stack([cc_re + ss_im, cc_im - ss_re])


def inverse_two(spec, k1_start, period):
    classes = spec.shape[2]
    length = spec.shape[3]
    cos_a, sin_a = phase(
        jnp.arange(length, dtype=jnp.int32), jnp.arange(length, dtype=jnp.int32), length
    )
    real_in, imag_in = (spec[0], spec[1])
    cc_re = jnp.einsum("nq,bkqc->bknc", cos_a, real_in, precision=HIGH)
    cc_im = jnp.einsum("nq,bkqc->bknc", cos_a, imag_in, precision=HIGH)
    ss_re = jnp.einsum("nq,bkqc->bknc", sin_a, real_in, precision=HIGH)
    ss_im = jnp.einsum("nq,bkqc->bknc", sin_a, imag_in, precision=HIGH)
    back_re = cc_re - ss_im
    back_im = cc_im + ss_re
    cos_b, sin_b = phase(
        k1_start + jnp.arange(classes, dtype=jnp.int32), jnp.arange(length, dtype=jnp.int32), period
    )
    tw_re = cos_b[None, :, :, None]
    tw_im = sin_b[None, :, :, None]
    return jnp.stack([back_re * tw_re - back_im * tw_im, back_re * tw_im + back_im * tw_re])


def inverse_one(spec, period):
    classes = spec.shape[2]
    count = classes // 2
    cos_a, sin_a = phase(
        jnp.arange(count, dtype=jnp.int32), jnp.arange(classes, dtype=jnp.int32), classes
    )
    real_out = jnp.einsum("nk,bkmc->bnmc", cos_a, spec[0], precision=HIGH)
    real_out = real_out - jnp.einsum("nk,bkmc->bnmc", sin_a, spec[1], precision=HIGH)
    return real_out / period


def products(spec):
    filt_re, filt_im = (spec[0, 0], spec[1, 0])
    prod_re, prod_im = (spec[0, 1], spec[1, 1])
    grad_re, grad_im = (spec[0, 2], spec[1, 2])
    out_re = jnp.stack(
        [
            filt_re * prod_re - filt_im * prod_im,
            filt_re * grad_re + filt_im * grad_im,
            prod_re * grad_re + prod_im * grad_im,
        ]
    )
    out_im = jnp.stack(
        [
            filt_re * prod_im + filt_im * prod_re,
            filt_re * grad_im - filt_im * grad_re,
            prod_re * grad_im - prod_im * grad_re,
        ]
    )
    return jnp.stack([out_re, out_im])


def shards(inputs, short_weight, taps, w_out, grad_out):
    rows = inputs.shape[1]
    span = short_weight.shape[1]
    count = lax.axis_size("ctx")
    where = lax.axis_index("ctx")
    period = 2 * count * rows
    scale = 1.0 / math.sqrt(count * rows)
    prior = shifted(inputs[:, rows - (span - 1) :, :], "ctx", 1)
    extended = jnp.concatenate([prior, inputs], axis=1).astype(jnp.float32)
    mixed = jnp.zeros((3, rows, inputs.shape[2]), jnp.float32)
    for j in range(span):
        mixed = (
            mixed + short_weight[:, j][:, None, :] * extended[:, span - 1 - j : span - 1 - j + rows]
        )
    query, key_s, value = (mixed[0], mixed[1], mixed[2])
    product = key_s * value
    filt = taps * scale
    columns = w_out
    gated_grad = lax.dot_general(
        lax.all_gather(grad_out, "tp", axis=1, tiled=True),
        columns,
        (((1,), (1,)), ((), ())),
        preferred_element_type=jnp.float32,
    )
    dy = gated_grad * query
    stacked = jnp.stack([filt, product, dy])
    width = rows // count
    blocks = stacked.reshape(3, count, width, stacked.shape[2])
    columns = section_one(
        lax.all_to_all(blocks, "ctx", split_axis=1, concat_axis=1, tiled=True),
        n2_start=where * width,
        period=period,
    )
    spec = section_two(lax.all_to_all(columns, "ctx", split_axis=2, concat_axis=3, tiled=True))
    back = inverse_two(products(spec), where * spec.shape[2], period)
    parted = inverse_one(
        lax.all_to_all(back, "ctx", split_axis=3, concat_axis=2, tiled=True), period=period
    )
    result = lax.all_to_all(parted, "ctx", split_axis=1, concat_axis=1, tiled=True).reshape(
        3, rows, stacked.shape[2]
    )
    conv_out, dz, raw = (result[0], result[1], result[2])
    dmixed = jnp.stack([gated_grad * conv_out, dz * value, dz * key_s])
    following = shifted(dmixed[:, : span - 1, :].astype(jnp.bfloat16), "ctx", -1).astype(
        jnp.float32
    )
    dext = jnp.concatenate([dmixed, following], axis=1)
    inputs_grad = jnp.zeros_like(dmixed)
    sums = []
    for j in range(span):
        inputs_grad = inputs_grad + short_weight[:, j][:, None, :] * dext[:, j : j + rows]
        sums.append(jnp.sum(dmixed * extended[:, span - 1 - j : span - 1 - j + rows], axis=1))
    short_grad = lax.psum(jnp.stack(sums, axis=1), "ctx") * scale
    return (inputs_grad.astype(jnp.bfloat16), raw * scale, short_grad)


def log2(x):
    return jnp.log(x) * (1.0 / math.log(2.0))


def encode(x):
    peak = jnp.maximum(jnp.max(jnp.abs(x), axis=0, keepdims=True), 1e-30)
    power = jnp.ceil(log2(peak))
    level = jnp.floor(jnp.abs(x) * (jnp.exp2(-power) * TOP) + 0.5)
    level = jnp.minimum(level, TOP)
    octave = jnp.floor(level * (1.0 / 128.0))
    size = jnp.exp2(octave - 123.0) * (1.0 + (level - octave * 128.0) * (1.0 / 128.0))
    return jnp.where(x < 0.0, -size, size).astype(jnp.bfloat16), power


def decode(words, power):
    words = words.astype(jnp.float32)
    size = jnp.abs(words)
    octave = jnp.floor(log2(size) + 0.0014)
    part = jnp.floor(size * jnp.exp2(-octave) * 128.0 + 0.5)
    level = octave * 128.0 + part + (123.0 * 128.0 - 128.0)
    return jnp.where(words < 0.0, -level, level) * (jnp.exp2(power.astype(jnp.float32)) / TOP)


def rows_of(powers):
    row = lax.broadcasted_iota(jnp.int32, (16, powers[0].shape[1]), 0)
    return jnp.where(row == 0, powers[0], powers[-1]).astype(jnp.bfloat16)


def split(x):
    high = x.astype(jnp.bfloat16)
    return high, (x - high.astype(jnp.float32)).astype(jnp.bfloat16)


def product3(m_high, m_low, x):
    x_high, x_low = split(x)
    dot = lambda a, b: jnp.dot(a, b, preferred_element_type=jnp.float32)
    return dot(m_high, x_high) + (dot(m_low, x_high) + dot(m_high, x_low))


def times_root(z, k, count, sign):
    re, im = z
    k = k % count
    if 8 * k % count == 0:
        turn = 8 * k // count
        if turn % 2 == 0:
            for _ in range(turn // 2):
                re, im = (im, -re) if sign < 0 else (-im, re)
            return re, im
    c, s = math.cos(2 * math.pi * k / count), sign * math.sin(2 * math.pi * k / count)
    if 8 * k % count == 0:
        r = abs(c)
        if (c > 0) == (s > 0):
            out = (re - im) * r, (re + im) * r
        else:
            out = (re + im) * r, (im - re) * r
        return out if c > 0 else (-out[0], -out[1])
    return re * c - im * s, re * s + im * c


def small_dft(z, sign):
    count = len(z)
    if count == 1:
        return z
    even, odd = small_dft(z[0::2], sign), small_dft(z[1::2], sign)
    odd = [times_root(v, k, count, sign) for k, v in enumerate(odd)]
    return [(a[0] + b[0], a[1] + b[1]) for a, b in zip(even, odd)] + [
        (a[0] - b[0], a[1] - b[1]) for a, b in zip(even, odd)
    ]


def matrices(length):
    radix = length // FINE
    k = np.arange(FINE)[None, :, None] + 0.25
    n = radix * np.arange(FINE)[None, None, :] + np.arange(radix)[:, None, None]
    angle = -2.0 * np.pi * k * n / length
    forward = np.concatenate([np.cos(angle), np.sin(angle)], axis=1).astype(np.float32)

    def halves(m):
        high = m.astype(jnp.bfloat16)
        return np.stack([high, (m - high.astype(np.float32)).astype(jnp.bfloat16)])

    return halves(forward), halves(np.ascontiguousarray(forward.transpose(0, 2, 1)))


def greet():
    me, count = lax.axis_index("ctx"), lax.axis_size("ctx")
    line, lines = lax.axis_index("tp"), lax.axis_size("tp")
    barrier = pltpu.get_barrier_semaphore()
    for s in range(1, count):
        peer = {"ctx": lax.rem(me + s, count)}
        pl.semaphore_signal(barrier, inc=1, device_id=peer, device_id_type=MESH)
    for s in range(1, lines):
        peer = {"tp": lax.rem(line + s, lines)}
        pl.semaphore_signal(barrier, inc=1, device_id=peer, device_id_type=MESH)
    pl.semaphore_wait(barrier, count + lines - 2)


def remote(src, dst, send_sem, recv_sem, peer):
    return pltpu.make_async_remote_copy(
        src_ref=src,
        dst_ref=dst,
        send_sem=send_sem,
        recv_sem=recv_sem,
        device_id=peer,
        device_id_type=MESH,
    )


def operator_kernel(
    count, lines, span, scale,
    x_ref, sw_ref, taps_ref, w_hbm, go_ref, f_hbm, ft_hbm,
    ig_ref, tg_ref, sg_ref,
    w_ref, f_ref, ft_ref, go_all, ext, mix, gg, dm, xs, ys,
    pair_out, pair_in, one_out, one_in, halo_out, halo_in, parts, parts_in, total,
    local_sem, go_sem, halo_sem, send_sem, recv_sem,
):
    rows, width = taps_ref.shape
    lanes = width // count
    length = rows * count
    radix = length // FINE
    keep = span - 1
    me, line = lax.axis_index("ctx"), lax.axis_index("tp")
    group = max(1, FINE // lanes)
    groups = count // group

    def group_at(j):
        return lax.rem(lax.div(me, group) + j, groups)

    def w_load(j):
        at = pl.ds(pl.multiple_of(group_at(j) * group * lanes, lanes), group * lanes)
        return pltpu.make_async_copy(w_hbm.at[at], w_ref.at[at], local_sem.at[j])

    f_loads = [
        pltpu.make_async_copy(f_hbm, f_ref, local_sem.at[groups]),
        pltpu.make_async_copy(ft_hbm, ft_ref, local_sem.at[groups + 1]),
    ]
    for j in range(groups):
        w_load(j).start()
    for load in f_loads:
        load.start()

    for b in range(3):
        ext[b, 8:, :] = x_ref[b].astype(jnp.float32)
        halo_out[0, b * keep : (b + 1) * keep, :] = ext[b, 8 + rows - keep :, :]
    go_all[line] = go_ref[...]
    parts[...] = jnp.zeros_like(parts)
    greet()

    def halo(way, peer):
        return remote(
            halo_out.at[way], halo_in.at[way], halo_sem.at[way, 0], halo_sem.at[way, 1],
            {"ctx": peer},
        )

    def go_copy(owner, s, peer):
        return remote(
            go_ref, go_all.at[owner], go_sem.at[0, s], go_sem.at[1, s], {"tp": peer}
        )

    down = halo(0, lax.rem(me + 1, count))
    down.start()
    for s in range(1, lines):
        go_copy(line, s, lax.rem(line + s, lines)).start()

    def columns(d):
        return pl.ds(pl.multiple_of(d * lanes, lanes), lanes)

    def block_rows(d):
        return pl.ds(pl.multiple_of(d * rows, rows), rows)

    def sending(src, dst, phase, peer):
        return remote(
            src.at[peer], dst.at[me], send_sem.at[phase, peer], recv_sem.at[phase, me],
            {"ctx": peer},
        )

    def landing(src, dst, phase, peer):
        return remote(
            src.at[peer], dst.at[peer], send_sem.at[phase, peer], recv_sem.at[phase, peer],
            {"ctx": peer},
        )

    def fill(buf, d, values):
        powers = []
        for a, x in enumerate(values):
            words, power = encode(x)
            buf[d, pl.ds(a * rows, rows), :] = words
            powers.append(power)
        buf[d, pl.ds(len(values) * rows, 16), :] = rows_of(powers)

    def read(src, dst, phase, s, many):
        d = lax.rem(me + count - s, count)
        if s:
            landing(src, dst, phase, d).wait_recv()
        block = src[d] if s == 0 else dst[d]
        powers = block[many * rows :].astype(jnp.float32)
        return d, [
            (block[a * rows : (a + 1) * rows], powers[a : a + 1]) for a in range(many)
        ]

    order = list(range(1, count)) + [0]

    down.wait_recv()
    for b in range(3):
        got = halo_in[0, b * keep : (b + 1) * keep, :]
        ext[b, 8 - keep : 8, :] = jnp.where(me == 0, jnp.zeros_like(got), got)

    def mixing(c):
        at = columns(c)
        for b in range(3):
            value = jnp.zeros((rows, lanes), jnp.float32)
            for j in range(span):
                tap = sw_ref[b * span + j : b * span + j + 1, at]
                value = value + tap * ext[b, pl.ds(8 - j, rows), at]
            mix[b, :, at] = value

    for s in order:
        d = lax.rem(me + s, count)
        mixing(d)
        fill(pair_out.at[0], d, [taps_ref[:, columns(d)], mix[1, :, columns(d)] * mix[2, :, columns(d)]])
        if s:
            sending(pair_out.at[0], pair_in.at[0], 0, d).start()

    for s in range(1, lines):
        owner = lax.rem(line + lines - s, lines)
        go_copy(owner, s, owner).wait_recv()
    features = go_ref.shape[1]
    for j in range(groups):
        w_load(j).wait()
        at = pl.ds(pl.multiple_of(group_at(j) * group * lanes, lanes), group * lanes)
        value = jnp.zeros((rows, group * lanes), jnp.float32)
        for t in range(lines):
            value = value + lax.dot_general(
                go_all[t],
                w_ref[at, t * features : (t + 1) * features],
                (((1,), (1,)), ((), ())),
                preferred_element_type=jnp.float32,
            )
        gg[:, at] = value
        for i in range(group):
            d = group_at(j) * group + i
            fill(one_out.at[0], d, [gg[:, columns(d)] * mix[0, :, columns(d)]])

            @pl.when(d != me)
            def _():
                sending(one_out.at[0], one_in.at[0], 1, d).start()

    def forward(first, last):
        cols = pl.ds(first * lanes, (last - first) * lanes)
        for n2 in range(radix):
            x = [xs[a, pl.ds(n2, FINE, stride=radix), :] for a in range(first, last)]
            x = x[0] if len(x) == 1 else jnp.concatenate(x, axis=1)
            ys[n2, :, cols] = product3(f_ref[0, n2], f_ref[1, n2], x)

    def inverse(first, last):
        cols = pl.ds(first * lanes, (last - first) * lanes)
        for n2 in range(radix):
            x = product3(ft_ref[0, n2], ft_ref[1, n2], ys[n2, :, cols])
            for a in range(first, last):
                xs[a, pl.ds(n2, FINE, stride=radix), :] = x[
                    :, (a - first) * lanes : (a - first + 1) * lanes
                ]

    def load_tile(row, a):
        cols = pl.ds(a * lanes, lanes)
        return [
            (ys[n2, pl.ds(row, 8), cols], ys[n2, pl.ds(FINE + row, 8), cols])
            for n2 in range(radix)
        ]

    def save_tile(row, a, z):
        cols = pl.ds(a * lanes, lanes)
        for n2, (re, im) in enumerate(z):
            ys[n2, pl.ds(row, 8), cols] = re
            ys[n2, pl.ds(FINE + row, 8), cols] = im

    for s in range(count):
        d, blocks = read(pair_out.at[0], pair_in.at[0], 0, s, 2)
        for a in range(2):
            xs[a, block_rows(d), :] = decode(*blocks[a])
    for load in f_loads:
        load.wait()
    forward(0, 2)

    def spectra(t, _):
        row = pl.multiple_of(t * 8, 8)
        for a in range(2):
            save_tile(row, a, small_dft(load_tile(row, a), -1))
        return 0

    lax.fori_loop(0, FINE // 8, spectra, 0)

    for s in range(count):
        d, blocks = read(one_out.at[0], one_in.at[0], 1, s, 1)
        xs[2, block_rows(d), :] = decode(*blocks[0])
    forward(2, 3)

    def products(t, _):
        row = pl.multiple_of(t * 8, 8)
        filt, prod = load_tile(row, 0), load_tile(row, 1)
        grad = small_dft(load_tile(row, 2), -1)
        joined = [[], [], []]
        for (fr, fi), (pr, pi), (gr, gi) in zip(filt, prod, grad):
            joined[0].append((fr * pr - fi * pi, fr * pi + fi * pr))
            joined[1].append((fr * gr + fi * gi, fr * gi - fi * gr))
            joined[2].append((pr * gr + pi * gi, pr * gi - pi * gr))
        for a in range(3):
            save_tile(row, a, small_dft(joined[a], 1))
        return 0

    lax.fori_loop(0, FINE // 8, products, 0)

    inverse(0, 2)
    for s in order:
        d = lax.rem(me + s, count)
        fill(pair_out.at[1], d, [xs[a, block_rows(d), :] for a in range(2)])
        if s:
            sending(pair_out.at[1], pair_in.at[1], 2, d).start()
    inverse(2, 3)
    for s in order:
        d = lax.rem(me + s, count)
        fill(one_out.at[1], d, [xs[2, block_rows(d), :]])
        if s:
            sending(one_out.at[1], one_in.at[1], 3, d).start()

    factor = scale / length
    for s in range(count):
        d, blocks = read(pair_out.at[1], pair_in.at[1], 2, s, 2)
        at = columns(d)
        conv_out, dz = decode(*blocks[0]) * factor, decode(*blocks[1]) * factor
        for b, value in enumerate((gg[:, at] * conv_out, dz * mix[2, :, at], dz * mix[1, :, at])):
            dm[b, 0:rows, at] = value
            halo_out[1, b * keep : (b + 1) * keep, at] = value[:keep]
            for j in range(span):
                parts[d, b * span + j : b * span + j + 1, :] = jnp.sum(
                    value * ext[b, pl.ds(8 - j, rows), at], axis=0, keepdims=True
                )
        if s:
            sending(parts, parts_in, 4, d).start()
    up = halo(1, lax.rem(me + count - 1, count))
    up.start()
    value = parts[me]
    for s in range(1, count):
        d = lax.rem(me + count - s, count)
        landing(parts, parts_in, 4, d).wait_recv()
        value = value + parts_in[d]
    total[...] = value * scale
    sg_ref[me] = value * scale

    def sharing(peer, slot):
        return remote(
            total, sg_ref.at[slot], send_sem.at[5, peer], recv_sem.at[5, slot], {"ctx": peer}
        )

    for s in range(1, count):
        sharing(lax.rem(me + s, count), me).start()

    up.wait_recv()
    for b in range(3):
        got = halo_in[1, b * keep : (b + 1) * keep, :]
        dm[b, rows : rows + keep, :] = jnp.where(me == count - 1, jnp.zeros_like(got), got)

    def finish(c, _):
        at = columns(c)
        for b in range(3):
            value = jnp.zeros((rows, lanes), jnp.float32)
            for j in range(span):
                tap = sw_ref[b * span + j : b * span + j + 1, at]
                value = value + tap * dm[b, pl.ds(j, rows), at]
            ig_ref[b, :, at] = value.astype(jnp.bfloat16)
        return 0

    lax.fori_loop(0, count, finish, 0)
    for s in range(count):
        d, blocks = read(one_out.at[1], one_in.at[1], 3, s, 1)
        tg_ref[:, columns(d)] = decode(*blocks[0]) * factor
    for s in range(1, count):
        d = lax.rem(me + count - s, count)
        sharing(d, d).wait_recv()

    down.wait_send()
    up.wait_send()
    for s in range(1, lines):
        go_copy(line, s, lax.rem(line + s, lines)).wait_send()
    for s in range(1, count):
        d = lax.rem(me + s, count)
        sending(pair_out.at[0], pair_in.at[0], 0, d).wait_send()
        sending(one_out.at[0], one_in.at[0], 1, d).wait_send()
        sending(pair_out.at[1], pair_in.at[1], 2, d).wait_send()
        sending(one_out.at[1], one_in.at[1], 3, d).wait_send()
        sending(parts, parts_in, 4, d).wait_send()
        sharing(d, me).wait_send()


def channel_shards(inputs, short_weight, taps, w_out, grad_out):
    rows, width = taps.shape
    span = short_weight.shape[1]
    count, lines = lax.axis_size("ctx"), lax.axis_size("tp")
    lanes, length = width // count, rows * count
    radix, groups = length // FINE, count // max(1, FINE // lanes)
    scale = 1.0 / math.sqrt(length)
    forward, backward = matrices(length)
    vmem, anywhere = pl.BlockSpec(memory_space=pltpu.VMEM), pl.BlockSpec(memory_space=pl.ANY)
    f32, bf16 = jnp.float32, jnp.bfloat16
    sums = (count, -(-3 * span // 8) * 8, lanes)
    inputs_grad, taps_grad, short_grad = pl.pallas_call(
        functools.partial(operator_kernel, count, lines, span, scale),
        out_shape=[
            jax.ShapeDtypeStruct(inputs.shape, bf16),
            jax.ShapeDtypeStruct(taps.shape, f32),
            jax.ShapeDtypeStruct(sums, f32),
        ],
        in_specs=[vmem, vmem, vmem, anywhere, vmem, anywhere, anywhere],
        out_specs=[vmem] * 3,
        scratch_shapes=[
            pltpu.VMEM(w_out.shape, bf16),
            pltpu.VMEM(forward.shape, bf16),
            pltpu.VMEM(backward.shape, bf16),
            pltpu.VMEM((lines,) + grad_out.shape, bf16),
            pltpu.VMEM((3, rows + 8, width), f32),
            pltpu.VMEM((3, rows, width), f32),
            pltpu.VMEM((rows, width), f32),
            pltpu.VMEM((3, rows + 8, width), f32),
            pltpu.VMEM((3, length, lanes), f32),
            pltpu.VMEM((radix, 2 * FINE, 3 * lanes), f32),
            pltpu.VMEM((2, count, 2 * rows + 16, lanes), bf16),
            pltpu.VMEM((2, count, 2 * rows + 16, lanes), bf16),
            pltpu.VMEM((2, count, rows + 16, lanes), bf16),
            pltpu.VMEM((2, count, rows + 16, lanes), bf16),
            pltpu.VMEM((2, -(-3 * (span - 1) // 8) * 8, width), f32),
            pltpu.VMEM((2, -(-3 * (span - 1) // 8) * 8, width), f32),
            pltpu.VMEM(sums, f32),
            pltpu.VMEM(sums, f32),
            pltpu.VMEM(sums[1:], f32),
            pltpu.SemaphoreType.DMA((groups + 2,)),
            pltpu.SemaphoreType.DMA((2, lines)),
            pltpu.SemaphoreType.DMA((2, 2)),
            pltpu.SemaphoreType.DMA((6, count)),
            pltpu.SemaphoreType.DMA((6, count)),
        ],
        compiler_params=pltpu.CompilerParams(
            collective_id=0, has_side_effects=True, vmem_limit_bytes=62 * 2**20
        ),
        cost_estimate=pl.CostEstimate(
            flops=2 * rows * width * w_out.shape[1], bytes_accessed=2 * w_out.size, transcendentals=0
        ),
        name="operator_backward",
    )(
        inputs,
        short_weight.reshape(3 * span, width),
        taps,
        w_out,
        grad_out,
        jnp.asarray(forward),
        jnp.asarray(backward),
    )
    short_grad = short_grad.transpose(1, 0, 2).reshape(sums[1], width)[: 3 * span]
    return inputs_grad, taps_grad, short_grad.reshape(3, span, width)


def any_shards(inputs, short_weight, taps, w_out, grad_out):
    rows, width = taps.shape
    count = lax.axis_size("ctx")
    whole_tiles = rows % 16 == 0 and width % (128 * count) == 0 and rows * count == 8 * FINE
    plan = channel_shards if whole_tiles else shards
    return plan(inputs, short_weight, taps, w_out, grad_out)


def solution(mesh):
    return jax.shard_map(
        any_shards,
        mesh=mesh,
        in_specs=(
            P(None, "ctx", "tp"),
            P(None, None, "tp"),
            P("ctx", "tp"),
            P("tp", None),
            P("ctx", "tp"),
        ),
        out_specs=(P(None, "ctx", "tp"), P("ctx", "tp"), P(None, None, "tp")),
        check_vma=False,
    )
```

```python
import functools
import math

import jax
import jax.numpy as jnp
import numpy as np
from jax import lax
from jax.experimental import pallas as pl
from jax.experimental.pallas import tpu as pltpu
from jax.sharding import PartitionSpec as P

HIGH = lax.Precision.HIGHEST
MESH = pl.DeviceIdType.MESH
FINE = 256
TOP = 248.0 * 128.0 - 1.0


def shifted(x, axis, by):
    peers = lax.axis_size(axis)
    pairs = [(i, i + by) for i in range(peers) if 0 <= i + by < peers]
    return lax.ppermute(x, axis, pairs)


def phase(left_idx, right_idx, period):
    turns = left_idx[:, None] * right_idx[None, :] % period
    angle = turns.astype(jnp.float32) * (2.0 * math.pi / period)
    return (jnp.cos(angle), jnp.sin(angle))


def section_one(blocks, n2_start, period):
    count = blocks.shape[1]
    width = blocks.shape[2]
    cos_a, sin_a = phase(
        jnp.arange(2 * count, dtype=jnp.int32), jnp.arange(count, dtype=jnp.int32), 2 * count
    )
    real_part = jnp.einsum("kn,bnmc->bkmc", cos_a, blocks, precision=HIGH)
    imag_part = -jnp.einsum("kn,bnmc->bkmc", sin_a, blocks, precision=HIGH)
    cos_b, sin_b = phase(
        jnp.arange(2 * count, dtype=jnp.int32),
        n2_start + jnp.arange(width, dtype=jnp.int32),
        period,
    )
    tw_re = cos_b[None, :, :, None]
    tw_im = -sin_b[None, :, :, None]
    return jnp.stack([real_part * tw_re - imag_part * tw_im, real_part * tw_im + imag_part * tw_re])


def section_two(parts):
    length = parts.shape[3]
    cos_a, sin_a = phase(
        jnp.arange(length, dtype=jnp.int32), jnp.arange(length, dtype=jnp.int32), length
    )
    real_in, imag_in = (parts[0], parts[1])
    cc_re = jnp.einsum("qn,bknc->bkqc", cos_a, real_in, precision=HIGH)
    cc_im = jnp.einsum("qn,bknc->bkqc", cos_a, imag_in, precision=HIGH)
    ss_re = jnp.einsum("qn,bknc->bkqc", sin_a, real_in, precision=HIGH)
    ss_im = jnp.einsum("qn,bknc->bkqc", sin_a, imag_in, precision=HIGH)
    return jnp.stack([cc_re + ss_im, cc_im - ss_re])


def inverse_two(spec, k1_start, period):
    classes = spec.shape[2]
    length = spec.shape[3]
    cos_a, sin_a = phase(
        jnp.arange(length, dtype=jnp.int32), jnp.arange(length, dtype=jnp.int32), length
    )
    real_in, imag_in = (spec[0], spec[1])
    cc_re = jnp.einsum("nq,bkqc->bknc", cos_a, real_in, precision=HIGH)
    cc_im = jnp.einsum("nq,bkqc->bknc", cos_a, imag_in, precision=HIGH)
    ss_re = jnp.einsum("nq,bkqc->bknc", sin_a, real_in, precision=HIGH)
    ss_im = jnp.einsum("nq,bkqc->bknc", sin_a, imag_in, precision=HIGH)
    back_re = cc_re - ss_im
    back_im = cc_im + ss_re
    cos_b, sin_b = phase(
        k1_start + jnp.arange(classes, dtype=jnp.int32), jnp.arange(length, dtype=jnp.int32), period
    )
    tw_re = cos_b[None, :, :, None]
    tw_im = sin_b[None, :, :, None]
    return jnp.stack([back_re * tw_re - back_im * tw_im, back_re * tw_im + back_im * tw_re])


def inverse_one(spec, period):
    classes = spec.shape[2]
    count = classes // 2
    cos_a, sin_a = phase(
        jnp.arange(count, dtype=jnp.int32), jnp.arange(classes, dtype=jnp.int32), classes
    )
    real_out = jnp.einsum("nk,bkmc->bnmc", cos_a, spec[0], precision=HIGH)
    real_out = real_out - jnp.einsum("nk,bkmc->bnmc", sin_a, spec[1], precision=HIGH)
    return real_out / period


def products(spec):
    filt_re, filt_im = (spec[0, 0], spec[1, 0])
    prod_re, prod_im = (spec[0, 1], spec[1, 1])
    grad_re, grad_im = (spec[0, 2], spec[1, 2])
    out_re = jnp.stack(
        [
            filt_re * prod_re - filt_im * prod_im,
            filt_re * grad_re + filt_im * grad_im,
            prod_re * grad_re + prod_im * grad_im,
        ]
    )
    out_im = jnp.stack(
        [
            filt_re * prod_im + filt_im * prod_re,
            filt_re * grad_im - filt_im * grad_re,
            prod_re * grad_im - prod_im * grad_re,
        ]
    )
    return jnp.stack([out_re, out_im])


def shards(inputs, short_weight, taps, w_out, grad_out):
    rows = inputs.shape[1]
    span = short_weight.shape[1]
    count = lax.axis_size("ctx")
    where = lax.axis_index("ctx")
    period = 2 * count * rows
    scale = 1.0 / math.sqrt(count * rows)
    prior = shifted(inputs[:, rows - (span - 1) :, :], "ctx", 1)
    extended = jnp.concatenate([prior, inputs], axis=1).astype(jnp.float32)
    mixed = jnp.zeros((3, rows, inputs.shape[2]), jnp.float32)
    for j in range(span):
        mixed = (
            mixed + short_weight[:, j][:, None, :] * extended[:, span - 1 - j : span - 1 - j + rows]
        )
    query, key_s, value = (mixed[0], mixed[1], mixed[2])
    product = key_s * value
    filt = taps * scale
    columns = w_out
    gated_grad = lax.dot_general(
        lax.all_gather(grad_out, "tp", axis=1, tiled=True),
        columns,
        (((1,), (1,)), ((), ())),
        preferred_element_type=jnp.float32,
    )
    dy = gated_grad * query
    stacked = jnp.stack([filt, product, dy])
    width = rows // count
    blocks = stacked.reshape(3, count, width, stacked.shape[2])
    columns = section_one(
        lax.all_to_all(blocks, "ctx", split_axis=1, concat_axis=1, tiled=True),
        n2_start=where * width,
        period=period,
    )
    spec = section_two(lax.all_to_all(columns, "ctx", split_axis=2, concat_axis=3, tiled=True))
    back = inverse_two(products(spec), where * spec.shape[2], period)
    parted = inverse_one(
        lax.all_to_all(back, "ctx", split_axis=3, concat_axis=2, tiled=True), period=period
    )
    result = lax.all_to_all(parted, "ctx", split_axis=1, concat_axis=1, tiled=True).reshape(
        3, rows, stacked.shape[2]
    )
    conv_out, dz, raw = (result[0], result[1], result[2])
    dmixed = jnp.stack([gated_grad * conv_out, dz * value, dz * key_s])
    following = shifted(dmixed[:, : span - 1, :].astype(jnp.bfloat16), "ctx", -1).astype(
        jnp.float32
    )
    dext = jnp.concatenate([dmixed, following], axis=1)
    inputs_grad = jnp.zeros_like(dmixed)
    sums = []
    for j in range(span):
        inputs_grad = inputs_grad + short_weight[:, j][:, None, :] * dext[:, j : j + rows]
        sums.append(jnp.sum(dmixed * extended[:, span - 1 - j : span - 1 - j + rows], axis=1))
    short_grad = lax.psum(jnp.stack(sums, axis=1), "ctx") * scale
    return (inputs_grad.astype(jnp.bfloat16), raw * scale, short_grad)


def log2(x):
    return jnp.log(x) * (1.0 / math.log(2.0))


def encode(x):
    peak = jnp.maximum(jnp.max(jnp.abs(x), axis=0, keepdims=True), 1e-30)
    power = jnp.ceil(log2(peak))
    level = jnp.floor(jnp.abs(x) * (jnp.exp2(-power) * TOP) + 0.5)
    level = jnp.minimum(level, TOP)
    octave = jnp.floor(level * (1.0 / 128.0))
    size = jnp.exp2(octave - 123.0) * (1.0 + (level - octave * 128.0) * (1.0 / 128.0))
    return jnp.where(x < 0.0, -size, size).astype(jnp.bfloat16), power


def decode(words, power):
    words = words.astype(jnp.float32)
    size = jnp.abs(words)
    octave = jnp.floor(log2(size) + 0.0014)
    part = jnp.floor(size * jnp.exp2(-octave) * 128.0 + 0.5)
    level = octave * 128.0 + part + (123.0 * 128.0 - 128.0)
    return jnp.where(words < 0.0, -level, level) * (jnp.exp2(power.astype(jnp.float32)) / TOP)


def split(x):
    high = x.astype(jnp.bfloat16)
    return high, (x - high.astype(jnp.float32)).astype(jnp.bfloat16)


def product3(m_high, m_low, x):
    x_high, x_low = split(x)
    dot = lambda a, b: jnp.dot(a, b, preferred_element_type=jnp.float32)
    return dot(m_high, x_high) + (dot(m_low, x_high) + dot(m_high, x_low))


def times_root(z, k, count, sign):
    re, im = z
    k = k % count
    if 8 * k % count == 0:
        turn = 8 * k // count
        if turn % 2 == 0:
            for _ in range(turn // 2):
                re, im = (im, -re) if sign < 0 else (-im, re)
            return re, im
    c, s = math.cos(2 * math.pi * k / count), sign * math.sin(2 * math.pi * k / count)
    if 8 * k % count == 0:
        r = abs(c)
        if (c > 0) == (s > 0):
            out = (re - im) * r, (re + im) * r
        else:
            out = (re + im) * r, (im - re) * r
        return out if c > 0 else (-out[0], -out[1])
    return re * c - im * s, re * s + im * c


def small_dft(z, sign):
    count = len(z)
    if count == 1:
        return z
    even, odd = small_dft(z[0::2], sign), small_dft(z[1::2], sign)
    odd = [times_root(v, k, count, sign) for k, v in enumerate(odd)]
    return [(a[0] + b[0], a[1] + b[1]) for a, b in zip(even, odd)] + [
        (a[0] - b[0], a[1] - b[1]) for a, b in zip(even, odd)
    ]


def matrices(length):
    radix = length // FINE
    k = np.arange(FINE)[None, :, None] + 0.25
    n = radix * np.arange(FINE)[None, None, :] + np.arange(radix)[:, None, None]
    angle = -2.0 * np.pi * k * n / length
    forward = np.concatenate([np.cos(angle), np.sin(angle)], axis=1).astype(np.float32)

    def halves(m):
        high = m.astype(jnp.bfloat16)
        return np.stack([high, (m - high.astype(np.float32)).astype(jnp.bfloat16)])

    return halves(forward), halves(np.ascontiguousarray(forward.transpose(0, 2, 1)))


def greet():
    me, count = lax.axis_index("ctx"), lax.axis_size("ctx")
    line, lines = lax.axis_index("tp"), lax.axis_size("tp")
    barrier = pltpu.get_barrier_semaphore()
    for s in range(1, count):
        peer = {"ctx": lax.rem(me + s, count)}
        pl.semaphore_signal(barrier, inc=1, device_id=peer, device_id_type=MESH)
    for s in range(1, lines):
        peer = {"tp": lax.rem(line + s, lines)}
        pl.semaphore_signal(barrier, inc=1, device_id=peer, device_id_type=MESH)
    pl.semaphore_wait(barrier, count + lines - 2)


def remote(src, dst, send_sem, recv_sem, peer):
    return pltpu.make_async_remote_copy(
        src_ref=src,
        dst_ref=dst,
        send_sem=send_sem,
        recv_sem=recv_sem,
        device_id=peer,
        device_id_type=MESH,
    )


def operator_kernel(
    count, lines, span, scale,
    x_ref, sw_ref, taps_ref, w_hbm, go_ref, f_hbm, ft_hbm,
    ig_ref, tg_ref, sg_ref,
    w_ref, f_ref, ft_ref, go_all, ext, mix, gg, dm, xs, ys,
    out_buf, in_buf, halo_out, halo_in, parts, parts_in, total,
    local_sem, go_sem, halo_sem, send_sem, recv_sem,
):
    rows, width = taps_ref.shape
    lanes = width // count
    length = rows * count
    radix = length // FINE
    keep = span - 1
    me, line = lax.axis_index("ctx"), lax.axis_index("tp")
    group = max(1, FINE // lanes)
    groups = count // group

    def group_at(j):
        return lax.rem(lax.div(me, group) + j, groups)

    def w_load(j):
        at = pl.ds(pl.multiple_of(group_at(j) * group * lanes, lanes), group * lanes)
        return pltpu.make_async_copy(w_hbm.at[at], w_ref.at[at], local_sem.at[j])

    f_loads = [
        pltpu.make_async_copy(f_hbm, f_ref, local_sem.at[groups]),
        pltpu.make_async_copy(ft_hbm, ft_ref, local_sem.at[groups + 1]),
    ]
    for j in range(groups):
        w_load(j).start()
    for load in f_loads:
        load.start()

    for b in range(3):
        ext[b, 8:, :] = x_ref[b].astype(jnp.float32)
        halo_out[0, b * keep : (b + 1) * keep, :] = ext[b, 8 + rows - keep :, :]
    go_all[line] = go_ref[...]
    parts[...] = jnp.zeros_like(parts)
    greet()

    def halo(way, peer):
        return remote(
            halo_out.at[way], halo_in.at[way], halo_sem.at[way, 0], halo_sem.at[way, 1],
            {"ctx": peer},
        )

    def go_copy(owner, s, peer):
        return remote(
            go_ref, go_all.at[owner], go_sem.at[0, s], go_sem.at[1, s], {"tp": peer}
        )

    down = halo(0, lax.rem(me + 1, count))
    down.start()
    for s in range(1, lines):
        go_copy(line, s, lax.rem(line + s, lines)).start()

    def columns(d):
        return pl.ds(pl.multiple_of(d * lanes, lanes), lanes)

    def block_rows(d):
        return pl.ds(pl.multiple_of(d * rows, rows), rows)

    def sending(src, dst, phase, peer):
        return remote(
            src.at[peer], dst.at[me], send_sem.at[phase, peer], recv_sem.at[phase, me],
            {"ctx": peer},
        )

    def landing(src, dst, phase, peer):
        return remote(
            src.at[peer], dst.at[peer], send_sem.at[phase, peer], recv_sem.at[phase, peer],
            {"ctx": peer},
        )

    def block_send(phase, d):
        return sending(out_buf.at[phase], in_buf.at[phase], phase, d)

    def fill(phase, d, value):
        words, power = encode(value)
        out_buf[phase, d, 0:rows, :] = words
        out_buf[phase, d, pl.ds(rows, 16), :] = jnp.broadcast_to(power, (16, lanes)).astype(
            jnp.bfloat16
        )

    def read(phase, s):
        d = lax.rem(me + count - s, count)
        if s:
            landing(out_buf.at[phase], in_buf.at[phase], phase, d).wait_recv()
        block = out_buf[phase, d] if s == 0 else in_buf[phase, d]
        return d, decode(block[:rows], block[rows:].astype(jnp.float32)[0:1])

    far = sorted(range(1, count), key=lambda s: -min(s, count - s))
    for s in far + [0]:
        d = lax.rem(me + s, count)
        fill(0, d, taps_ref[:, columns(d)])
        if s:
            block_send(0, d).start()

    down.wait_recv()
    for b in range(3):
        got = halo_in[0, b * keep : (b + 1) * keep, :]
        ext[b, 8 - keep : 8, :] = jnp.where(me == 0, jnp.zeros_like(got), got)

    def mixing(c):
        at = columns(c)
        for b in range(3):
            value = jnp.zeros((rows, lanes), jnp.float32)
            for j in range(span):
                tap = sw_ref[b, j : j + 1, at]
                value = value + tap * ext[b, pl.ds(8 - j, rows), at]
            mix[b, :, at] = value

    for s in far + [0]:
        d = lax.rem(me + s, count)
        mixing(d)
        fill(1, d, mix[1, :, columns(d)] * mix[2, :, columns(d)])
        if s:
            block_send(1, d).start()

    for s in range(1, lines):
        owner = lax.rem(line + lines - s, lines)
        go_copy(owner, s, owner).wait_recv()
    features = go_ref.shape[1]
    for j in range(groups):
        w_load(j).wait()
        at = pl.ds(pl.multiple_of(group_at(j) * group * lanes, lanes), group * lanes)
        value = jnp.zeros((rows, group * lanes), jnp.float32)
        for t in range(lines):
            value = value + lax.dot_general(
                go_all[t],
                w_ref[at, t * features : (t + 1) * features],
                (((1,), (1,)), ((), ())),
                preferred_element_type=jnp.float32,
            )
        gg[:, at] = value
        for i in range(group):
            d = group_at(j) * group + i
            fill(2, d, gg[:, columns(d)] * mix[0, :, columns(d)])

            @pl.when(d != me)
            def _():
                block_send(2, d).start()

    def forward(first, last):
        cols = pl.ds(first * lanes, (last - first) * lanes)
        for n2 in range(radix):
            x = [xs[a, pl.ds(n2, FINE, stride=radix), :] for a in range(first, last)]
            x = x[0] if len(x) == 1 else jnp.concatenate(x, axis=1)
            ys[n2, :, cols] = product3(f_ref[0, n2], f_ref[1, n2], x)

    def inverse(first, last):
        cols = pl.ds(first * lanes, (last - first) * lanes)
        for n2 in range(radix):
            x = product3(ft_ref[0, n2], ft_ref[1, n2], ys[n2, :, cols])
            for a in range(first, last):
                xs[a, pl.ds(n2, FINE, stride=radix), :] = x[
                    :, (a - first) * lanes : (a - first + 1) * lanes
                ]

    def load_tile(row, a):
        cols = pl.ds(a * lanes, lanes)
        return [
            (ys[n2, pl.ds(row, 8), cols], ys[n2, pl.ds(FINE + row, 8), cols])
            for n2 in range(radix)
        ]

    def save_tile(row, a, z):
        cols = pl.ds(a * lanes, lanes)
        for n2, (re, im) in enumerate(z):
            ys[n2, pl.ds(row, 8), cols] = re
            ys[n2, pl.ds(FINE + row, 8), cols] = im

    def collect(phase, a):
        for s in [0] + far:
            d, value = read(phase, s)
            xs[a, block_rows(d), :] = value

    def give_back(phase, a):
        inverse(a, a + 1)
        for s in far + [0]:
            d = lax.rem(me + s, count)
            fill(phase, d, xs[a, block_rows(d), :])
            if s:
                block_send(phase, d).start()

    def multiply(p, q):
        return [(a * c - b * d, a * d + b * c) for (a, b), (c, d) in zip(p, q)]

    def correlate(p, q):
        return [(a * c + b * d, a * d - b * c) for (a, b), (c, d) in zip(p, q)]

    collect(0, 0)
    collect(1, 1)
    for load in f_loads:
        load.wait()
    forward(0, 2)

    def early(t, _):
        row = pl.multiple_of(t * 8, 8)
        specs = [small_dft(load_tile(row, a), -1) for a in range(2)]
        for a in range(2):
            save_tile(row, a, specs[a])
        save_tile(row, 2, small_dft(multiply(*specs), 1))
        return 0

    lax.fori_loop(0, FINE // 8, early, 0)
    give_back(3, 2)
    collect(2, 2)
    forward(2, 3)

    def late(t, _):
        row = pl.multiple_of(t * 8, 8)
        grad = small_dft(load_tile(row, 2), -1)
        for a in range(2):
            save_tile(row, a, small_dft(correlate(load_tile(row, a), grad), 1))
        return 0

    lax.fori_loop(0, FINE // 8, late, 0)
    give_back(4, 0)
    give_back(5, 1)

    factor = scale / length

    def mixed_grad(b, d, value):
        at = columns(d)
        dm[b, 0:rows, at] = value
        halo_out[1, b * keep : (b + 1) * keep, at] = value[:keep]
        for j in range(span):
            parts[d, b * span + j : b * span + j + 1, :] = jnp.sum(
                value * ext[b, pl.ds(8 - j, rows), at], axis=0, keepdims=True
            )

    for s in [0] + far:
        d, value = read(3, s)
        mixed_grad(0, d, gg[:, columns(d)] * (value * factor))
    for s in [0] + far:
        d, value = read(4, s)
        value = value * factor
        mixed_grad(1, d, value * mix[2, :, columns(d)])
        mixed_grad(2, d, value * mix[1, :, columns(d)])
        if s:
            sending(parts, parts_in, 6, d).start()
    up = halo(1, lax.rem(me + count - 1, count))
    up.start()
    value = parts[me]
    for s in range(1, count):
        d = lax.rem(me + count - s, count)
        landing(parts, parts_in, 6, d).wait_recv()
        value = value + parts_in[d]
    total[...] = value * scale
    sg_ref[:, columns(me)] = value * scale

    def sharing(peer, slot):
        return remote(
            total, sg_ref.at[:, columns(slot)], send_sem.at[7, peer], recv_sem.at[7, slot],
            {"ctx": peer},
        )

    for s in range(1, count):
        sharing(lax.rem(me + s, count), me).start()

    up.wait_recv()
    for b in range(3):
        got = halo_in[1, b * keep : (b + 1) * keep, :]
        dm[b, rows : rows + keep, :] = jnp.where(me == count - 1, jnp.zeros_like(got), got)

    def finish(c, _):
        at = columns(c)
        for b in range(3):
            value = jnp.zeros((rows, lanes), jnp.float32)
            for j in range(span):
                tap = sw_ref[b, j : j + 1, at]
                value = value + tap * dm[b, pl.ds(j, rows), at]
            ig_ref[b, :, at] = value.astype(jnp.bfloat16)
        return 0

    lax.fori_loop(0, count, finish, 0)
    for s in [0] + far:
        d, value = read(5, s)
        tg_ref[:, columns(d)] = value * factor
    for s in range(1, count):
        d = lax.rem(me + count - s, count)
        sharing(d, d).wait_recv()

    down.wait_send()
    up.wait_send()
    for s in range(1, lines):
        go_copy(line, s, lax.rem(line + s, lines)).wait_send()
    for s in range(1, count):
        d = lax.rem(me + s, count)
        for phase in range(6):
            block_send(phase, d).wait_send()
        sending(parts, parts_in, 6, d).wait_send()
        sharing(d, me).wait_send()


def channel_shards(inputs, short_weight, taps, w_out, grad_out):
    rows, width = taps.shape
    span = short_weight.shape[1]
    count, lines = lax.axis_size("ctx"), lax.axis_size("tp")
    lanes, length = width // count, rows * count
    radix, groups = length // FINE, count // max(1, FINE // lanes)
    scale = 1.0 / math.sqrt(length)
    forward, backward = matrices(length)
    vmem, anywhere = pl.BlockSpec(memory_space=pltpu.VMEM), pl.BlockSpec(memory_space=pl.ANY)
    f32, bf16 = jnp.float32, jnp.bfloat16
    sums = (count, -(-3 * span // 8) * 8, lanes)
    inputs_grad, taps_grad, short_grad = pl.pallas_call(
        functools.partial(operator_kernel, count, lines, span, scale),
        out_shape=[
            jax.ShapeDtypeStruct(inputs.shape, bf16),
            jax.ShapeDtypeStruct(taps.shape, f32),
            jax.ShapeDtypeStruct((sums[1], width), f32),
        ],
        in_specs=[vmem, vmem, vmem, anywhere, vmem, anywhere, anywhere],
        out_specs=[vmem] * 3,
        scratch_shapes=[
            pltpu.VMEM(w_out.shape, bf16),
            pltpu.VMEM(forward.shape, bf16),
            pltpu.VMEM(backward.shape, bf16),
            pltpu.VMEM((lines,) + grad_out.shape, bf16),
            pltpu.VMEM((3, rows + 8, width), f32),
            pltpu.VMEM((3, rows, width), f32),
            pltpu.VMEM((rows, width), f32),
            pltpu.VMEM((3, rows + 8, width), f32),
            pltpu.VMEM((3, length, lanes), f32),
            pltpu.VMEM((radix, 2 * FINE, 3 * lanes), f32),
            pltpu.VMEM((6, count, rows + 16, lanes), bf16),
            pltpu.VMEM((6, count, rows + 16, lanes), bf16),
            pltpu.VMEM((2, -(-3 * (span - 1) // 8) * 8, width), f32),
            pltpu.VMEM((2, -(-3 * (span - 1) // 8) * 8, width), f32),
            pltpu.VMEM(sums, f32),
            pltpu.VMEM(sums, f32),
            pltpu.VMEM(sums[1:], f32),
            pltpu.SemaphoreType.DMA((groups + 2,)),
            pltpu.SemaphoreType.DMA((2, lines)),
            pltpu.SemaphoreType.DMA((2, 2)),
            pltpu.SemaphoreType.DMA((8, count)),
            pltpu.SemaphoreType.DMA((8, count)),
        ],
        compiler_params=pltpu.CompilerParams(
            collective_id=0, has_side_effects=True, vmem_limit_bytes=62 * 2**20
        ),
        cost_estimate=pl.CostEstimate(
            flops=2 * rows * width * w_out.shape[1], bytes_accessed=2 * w_out.size, transcendentals=0
        ),
        name="operator_backward",
    )(
        inputs,
        short_weight,
        taps,
        w_out,
        grad_out,
        jnp.asarray(forward),
        jnp.asarray(backward),
    )
    return inputs_grad, taps_grad, short_grad[: 3 * span].reshape(3, span, width)


def any_shards(inputs, short_weight, taps, w_out, grad_out):
    rows, width = taps.shape
    count = lax.axis_size("ctx")
    whole_tiles = rows % 16 == 0 and width % (128 * count) == 0 and rows * count == 8 * FINE
    plan = channel_shards if whole_tiles else shards
    return plan(inputs, short_weight, taps, w_out, grad_out)


def solution(mesh):
    return jax.shard_map(
        any_shards,
        mesh=mesh,
        in_specs=(
            P(None, "ctx", "tp"),
            P(None, None, "tp"),
            P("ctx", "tp"),
            P("tp", None),
            P("ctx", "tp"),
        ),
        out_specs=(P(None, "ctx", "tp"), P("ctx", "tp"), P(None, None, "tp")),
        check_vma=False,
    )
```
